32 devices in a mesh: grp: 2 (over y), row: 4 (over x, core), col: 4 (over z).
Axes of the slice: x: 2, y: 2, z: 4, core: 2. Of those that a mesh axis runs over, the one named last changes fastest.
Arguments:
- activations: bfloat16 [1280, 5120], P(('grp', 'row')), parts along dimension 0, may hold values from -6 to 6
- gradients: bfloat16 [1280, 5120], P(('grp', 'col')), parts along dimension 0, may hold values from -0.625 to 0.625
- input_basis: bfloat16 [10240, 5120], P(('grp', 'row'), 'col'), parts along dimension 0, may hold values from -0.078125 to 0.078125
- output_basis: bfloat16 [10240, 5120], P(('grp', 'col'), 'row'), parts along dimension 0, may hold values from -0.078125 to 0.078125
- seq_ids: int32 [1280], P('grp'), parts along dimension 0, may hold values from 0 to 3, never falling along the last dimension, each value on 1 to 320 neighbouring positions
Outputs:
- corrected: float32 [10240, 5120], P(('grp', 'col'), 'row'), parts along dimension 0
The draws below stay inside these ranges and needn't reach their ends.
There are 2 independent parts, one for each index of `grp`. The reference program is written for one: setup_inputs(seed, part) draws one part's arguments, and reference() takes and returns one part's arrays. A program takes and returns all parts, laid end to end along the dimension named above; each array names one. Nothing has to cross between parts.
Inputs may be any that keep to these rules, and one draw needn't show every extreme that they name: `seq_ids`: sequence ids never fall along the tokens; every sequence has at least one token and at most 320, one exactly 320.
All inputs are finite; a program needn't handle non-finite values.
Results may differ from the reference program's by a relative error of at most 0.0041.
Values may be sent and summed in bfloat16 or wider, within the bound.
No kernel may reach another device: no remote copies, remote signals or barrier semaphores. Data moves between devices by JAX's collectives and lax.ppermute only.
A program may use at most 128 MiB of HBM per device.

```python
import math
import jax
import jax.numpy as jnp
import numpy as np
from jax import lax

D = 5120
SEQS = 4
TOKENS = 640
MAXLEN = 320


def levels(key, dims, shards, low, top_value):
    def one(dim, shards_of):
        draws = jax.random.uniform(jax.random.fold_in(jax.random.fold_in(key, 6), dim), (shards_of,), jnp.float32, low / len(shards), top_value / len(shards))
        return jnp.repeat(jnp.exp(draws), dims[dim] // shards_of).reshape((-1,) + (1,) * (len(dims) - dim - 1))

    loudness = one(*shards[0])
    for cut in shards[1:]:
        loudness = loudness * one(*cut)
    return loudness


def length_profile(count, total, most, slope):
    loads = [(1 << 20) // math.isqrt(standing ** slope) + 1 for standing in range(2, count + 1)]
    surplus, holding = total - most - (count - 1), [1] * (count - 1)
    while surplus > 0:
        movable = [i for i in range(count - 1) if holding[i] < most]
        whole, budget = sum([loads[i] for i in movable]), surplus
        for i in movable:
            addition = min(most - holding[i], max(1, budget * loads[i] // whole), surplus)
            holding[i] = holding[i] + addition
            surplus = surplus - addition
    return np.array([most] + holding)


def uneven(own_key, count, total, most, slope):
    if count == 2:
        one = jax.random.randint(own_key, (), max(1, total - most), min(most, total - 1) + 1)
        return jnp.stack([one, total - one])
    tallies = jnp.asarray(length_profile(count, total, most, slope), jnp.int32)
    couples = (count - 1) // 2
    source_of, taker = tallies[1:1 + 2 * couples:2], tallies[2:2 + 2 * couples:2]
    slack = jnp.minimum(source_of - 1, most - taker)
    moved = jax.random.randint(jax.random.fold_in(own_key, 1), (couples,), 0, 1 << 20) % (slack + 1)
    tallies = tallies.at[1:1 + 2 * couples:2].set(source_of - moved).at[2:2 + 2 * couples:2].set(taker + moved)
    return tallies[jax.random.permutation(jax.random.fold_in(own_key, 2), count)]


def scatter_about(rng, extent, width, limit, shards=(), dtype=jnp.bfloat16):
    result = width * jax.random.normal(rng, extent, jnp.float32)
    if shards:
        result = result * levels(rng, extent, shards, -0.22, 0.18)
    return jnp.clip(result, -limit, limit).astype(dtype)


def setup_inputs(seed: int = 0, part: int = 0) -> dict:
    seeds = jax.random.split(jax.random.key(seed), 6)
    own_keys = jax.random.split(jax.random.fold_in(seeds[5], part), 6)
    activations = scatter_about(own_keys[0], (TOKENS, D), 1.0, 6.0, ((0, 4),))
    gradients = scatter_about(own_keys[1], (TOKENS, D), 0.04, 0.625, ((0, 4),))
    input_basis = scatter_about(own_keys[2], (D, D), D ** -0.5, 0.078125, ((0, 4), (1, 4)))
    output_basis = scatter_about(own_keys[3], (D, D), D ** -0.5, 0.078125, ((0, 4), (1, 4)))
    seq_ids = jnp.searchsorted(jnp.cumsum(uneven(own_keys[4], SEQS, TOKENS, MAXLEN, 0)), jnp.arange(TOKENS), side="right").astype(jnp.int32)
    return {"activations": activations, "gradients": gradients, "input_basis": input_basis, "output_basis": output_basis, "seq_ids": seq_ids}


def project(values, basis):
    return jnp.dot(values.astype(jnp.float32), basis.astype(jnp.float32), precision=lax.Precision.HIGHEST).astype(jnp.bfloat16)


def reference(activations, gradients, input_basis, output_basis, seq_ids):
    act_proj = project(activations, input_basis)
    grad_proj = project(gradients, output_basis)
    total_rows = seq_ids.shape[0]
    window = total_rows // 2
    total = jnp.zeros((act_proj.shape[1], grad_proj.shape[1]), jnp.float32)
    for seq in range(SEQS):
        first = jnp.sum((seq_ids < seq).astype(jnp.int32))
        begin = jnp.minimum(first, total_rows - window).astype(jnp.int32)
        left = lax.dynamic_slice_in_dim(act_proj, begin, window, 0)
        right = lax.dynamic_slice_in_dim(grad_proj, begin, window, 0)
        ids_here = lax.dynamic_slice_in_dim(seq_ids, begin, window, 0)
        masked = left.astype(jnp.float32) * (ids_here == seq).astype(jnp.float32)[:, None]
        seq_sum = jnp.dot(masked.T, right.astype(jnp.float32), precision=lax.Precision.HIGHEST)
        total = total + seq_sum * seq_sum
    return total / SEQS
```

```python
import jax
import jax.numpy as jnp
from jax import lax
from jax.sharding import PartitionSpec as P

SEQS = 4
BF16 = jnp.bfloat16
F32 = jnp.float32


def dot(values, piece):
    return jnp.dot(values, piece, preferred_element_type=F32)


def outer_sum(left, right):
    return lax.dot_general(
        left, right, (((0,), (0,)), ((), ())), preferred_element_type=F32
    )


def project_any(values, basis, axis):
    turned = lax.all_to_all(values, axis, split_axis=1, concat_axis=0, tiled=True)
    total = lax.psum_scatter(dot(turned, basis), axis, scatter_dimension=0, tiled=True)
    return lax.all_gather(total.astype(BF16), axis, axis=0, tiled=True)


def by_xor(values, axis, bits):
    return lax.ppermute(values, axis, [(i, i ^ bits) for i in range(4)])


def columns_of(values, index, width):
    return lax.dynamic_slice_in_dim(values, index * width, width, 1)


def place(blocks, indices, size):
    panel = jnp.zeros((4 * size, blocks[0].shape[1]), BF16)
    for block, index in zip(blocks, indices):
        panel = lax.dynamic_update_slice_in_dim(panel, block, index * size, 0)
    return panel


def project_square(values, basis):
    me = lax.axis_index("row")
    tokens, depth = values.shape[0], basis.shape[0]
    core = me % 2
    mine = columns_of(values, me, depth)
    for_core = columns_of(values, me ^ 1, depth)
    for_chip = columns_of(values, me // 2 ^ 1, 2 * depth)
    from_chip = by_xor(for_chip, "row", 2)
    from_core = by_xor(for_core, "row", 1)
    own = dot(mine, basis)
    part = dot(from_core, basis)
    near = own + by_xor(part, "row", 1)
    near_there = by_xor(near.astype(BF16), "row", 2)
    far_mine = columns_of(from_chip, core, depth)
    far_for_core = columns_of(from_chip, core ^ 1, depth)
    far_from_core = by_xor(far_for_core, "row", 1)
    far_part = dot(far_from_core, basis)
    far = dot(far_mine, basis) + by_xor(far_part, "row", 1)
    far_there = by_xor(far.astype(BF16), "row", 2)
    near = (near + far_there.astype(F32)).astype(BF16)
    far = (far + near_there.astype(F32)).astype(BF16)
    near_other = by_xor(near, "row", 1)
    far_other = by_xor(far, "row", 1)
    return place([near, far, near_other, far_other], [me, me ^ 2, me ^ 1, me ^ 3], tokens)


def project_line(values, basis):
    me = lax.axis_index("col")
    core = lax.axis_index("row") % 2
    tokens, depth = values.shape[0], basis.shape[0]
    half = tokens // 2
    right = me // 2
    inner = (me == 1) | (me == 2)
    own_half = lax.dynamic_slice_in_dim(values, core * half, half, 0)

    def fetch(index, send):
        piece = send(columns_of(own_half, index, depth))
        other = by_xor(piece, "row", 1)
        first = jnp.where(core == 0, piece, other)
        second = jnp.where(core == 0, other, piece)
        return jnp.concatenate([first, second], 0)

    beside = fetch(me ^ 1, lambda v: by_xor(v, "col", 1))
    across = fetch(3 - me, lambda v: by_xor(v, "col", 3))
    twice = fetch(me ^ 2, lambda v: by_xor(v, "col", 2))
    own = columns_of(values, me, depth)
    blocks = [
        jnp.where(inner, beside, own),
        jnp.where(inner, own, beside),
        jnp.where(inner, across, twice),
        jnp.where(inner, twice, across),
    ]
    parts = [dot(block, basis) for block in blocks]

    def step_outer(values, inward, outward):
        pairs = [(0, 1), (3, 2)] * inward + [(1, 0), (2, 3)] * outward
        return lax.ppermute(values, "col", pairs).astype(F32)

    arrived, sums, crossed = [], [], []
    for step in range(6):
        inward, outward = step < 4, step >= 2
        if outward:
            sent = (parts[5 - step] + crossed[step - 2]).astype(BF16)
        if inward:
            sent = jnp.where(inner, sent, parts[step].astype(BF16)) if outward else parts[step].astype(BF16)
        arrived.append(step_outer(sent, inward, outward))
        if inward:
            sums.append(parts[step] + arrived[step])
            crossed.append(
                lax.ppermute(sums[step].astype(BF16), "col", [(1, 2), (2, 1)]).astype(F32)
            )
    done = [
        jnp.where(inner, sums[j] + crossed[3 - j], parts[j] + arrived[5 - j]).astype(BF16)
        for j in range(4)
    ]
    return place(done, [jnp.where(right == 1, 3 - j, j) for j in range(4)], tokens)


def on_device(rows, cols, activations, gradients, input_basis, output_basis, seq_ids):
    if rows == 4 and cols == 4:
        grad_panel = project_line(gradients, output_basis)
        act_panel = project_square(activations, input_basis)
    else:
        act_panel = project_any(activations, input_basis, "row")
        grad_panel = project_any(gradients, output_basis, "col")
    total_rows = seq_ids.shape[0]
    window = total_rows // 2
    total = jnp.zeros((act_panel.shape[1], grad_panel.shape[1]), F32)
    for seq in range(SEQS):
        first = jnp.sum((seq_ids < seq).astype(jnp.int32))
        begin = jnp.minimum(first, total_rows - window)
        left = lax.dynamic_slice_in_dim(act_panel, begin, window, 0)
        right = lax.dynamic_slice_in_dim(grad_panel, begin, window, 0)
        ids_here = lax.dynamic_slice_in_dim(seq_ids, begin, window, 0)
        masked = left * (ids_here == seq).astype(BF16)[:, None]
        seq_sum = outer_sum(masked, right)
        total = total + seq_sum * seq_sum
    return total / SEQS


def solution(mesh):
    def body(*args):
        return on_device(mesh.shape["row"], mesh.shape["col"], *args)

    return jax.shard_map(
        body,
        mesh=mesh,
        in_specs=(
            P(("grp", "row"), None),
            P(("grp", "col"), None),
            P(("grp", "row"), "col"),
            P(("grp", "col"), "row"),
            P("grp"),
        ),
        out_specs=P(("grp", "col"), "row"),
        check_vma=False,
    )
```

```python
import functools

import jax
import jax.numpy as jnp
from jax import lax
from jax.experimental import pallas as pl
from jax.experimental.pallas import tpu as pltpu
from jax.sharding import PartitionSpec as P

SEQS = 4
BF16 = jnp.bfloat16
F32 = jnp.float32
NARROW = 256
VMEM_GRANT = 56 << 20


def dot(values, piece):
    return jnp.dot(values, piece, preferred_element_type=F32)


def outer_sum(left, right):
    return lax.dot_general(
        left, right, (((0,), (0,)), ((), ())), preferred_element_type=F32
    )


def project_any(values, basis, axis):
    turned = lax.all_to_all(values, axis, split_axis=1, concat_axis=0, tiled=True)
    total = lax.psum_scatter(dot(turned, basis), axis, scatter_dimension=0, tiled=True)
    return lax.all_gather(total.astype(BF16), axis, axis=0, tiled=True)


def correct_any(act_panel, grad_panel, seq_ids):
    total_rows = seq_ids.shape[0]
    window = total_rows // 2
    total = jnp.zeros((act_panel.shape[1], grad_panel.shape[1]), F32)
    for seq in range(SEQS):
        first = jnp.sum((seq_ids < seq).astype(jnp.int32))
        begin = jnp.minimum(first, total_rows - window)
        left = lax.dynamic_slice_in_dim(act_panel, begin, window, 0)
        right = lax.dynamic_slice_in_dim(grad_panel, begin, window, 0)
        ids_here = lax.dynamic_slice_in_dim(seq_ids, begin, window, 0)
        masked = left * (ids_here == seq).astype(BF16)[:, None]
        seq_sum = outer_sum(masked, right)
        total = total + seq_sum * seq_sum
    return total / SEQS


VMEM = pl.BlockSpec(memory_space=pltpu.VMEM)
SMEM = pl.BlockSpec(memory_space=pltpu.SMEM)
ANY = pl.BlockSpec(memory_space=pl.ANY)


def shaped(*shape, dtype=BF16):
    return jax.ShapeDtypeStruct(shape, dtype)


def columns_of(ref, rows, index, width):
    return ref.at[rows, pl.ds(pl.multiple_of(index * width, width), width)]


def copy_all(pairs, sems):
    copies = [pltpu.make_async_copy(src, dst, sems.at[i]) for i, (src, dst) in enumerate(pairs)]
    for copy in copies:
        copy.start()
    for copy in copies:
        copy.wait()


def cut_first(gradients, depth):
    tokens = gradients.shape[0]
    half = tokens // 2

    def kernel(grad, beside, own, token, sems):
        core, col = lax.axis_index("row") % 2, lax.axis_index("col")
        part = pl.ds(pl.multiple_of(core * half, half), half)
        token[...] = jnp.zeros_like(token)
        copy_all(
            [
                (columns_of(grad, part, col + 1 - 2 * (col % 2), depth), beside),
                (columns_of(grad, pl.ds(0, tokens), col, depth), own),
            ],
            sems,
        )

    return pl.pallas_call(
        kernel,
        out_shape=[shaped(half, depth), shaped(tokens, depth), shaped(8, 128, dtype=F32)],
        in_specs=[ANY],
        out_specs=[VMEM] * 3,
        scratch_shapes=[pltpu.SemaphoreType.DMA((2,))],
        compiler_params=pltpu.CompilerParams(vmem_limit_bytes=VMEM_GRANT),
    )(gradients)


def cut_rest(activations, gradients, depth, before):
    tokens = activations.shape[0]
    half = tokens // 2

    def kernel(act, grad, before, far, mine, across, twice, token, sems):
        token[...] = before[...]
        row, col = lax.axis_index("row"), lax.axis_index("col")
        core, chip = row % 2, row // 2
        whole = pl.ds(0, tokens)
        part = pl.ds(pl.multiple_of(core * half, half), half)
        left, right = pl.ds(0, depth), pl.ds(depth, depth)
        copy_all(
            [
                (columns_of(grad, part, 3 - col, depth), across),
                (columns_of(grad, part, col + 2 - 4 * (col // 2), depth), twice),
                (columns_of(act, whole, 2 - 2 * chip + core, depth), far.at[:, left]),
                (columns_of(act, whole, 3 - 2 * chip - core, depth), far.at[:, right]),
                (columns_of(act, whole, 2 * chip + core, depth), mine.at[:, left]),
                (columns_of(act, whole, 2 * chip + 1 - core, depth), mine.at[:, right]),
            ],
            sems,
        )

    return pl.pallas_call(
        kernel,
        out_shape=[shaped(tokens, 2 * depth)] * 2
        + [shaped(half, depth)] * 2
        + [shaped(8, 128, dtype=F32)],
        in_specs=[ANY] * 2 + [VMEM],
        out_specs=[VMEM] * 5,
        scratch_shapes=[pltpu.SemaphoreType.DMA((6,))],
        compiler_params=pltpu.CompilerParams(vmem_limit_bytes=48 << 20),
    )(activations, gradients, before)


def step(function, shapes, values, token, after=(), grant=16 << 20, flops=0):
    count, shapes = len(values), list(shapes) + [shaped(8, 128, dtype=F32)]

    def kernel(*refs):
        outs = function(*refs[:count])
        for ref, out in zip(refs[count + 1 + len(after) :], outs):
            ref[...] = out
        refs[-1][...] = refs[count][...]

    return pl.pallas_call(
        kernel,
        out_shape=shapes,
        in_specs=[VMEM] * (count + 1) + [ANY] * len(after),
        out_specs=[VMEM] * len(shapes),
        cost_estimate=pl.CostEstimate(flops=flops, bytes_accessed=0, transcendentals=0),
        compiler_params=pltpu.CompilerParams(vmem_limit_bytes=grant),
    )(*values, token, *after)


def is_inner():
    col = lax.axis_index("col")
    return (col == 1) | (col == 2)


def both_halves(here, there):
    first = lax.axis_index("row") % 2 == 0
    return jnp.concatenate([jnp.where(first, here, there), jnp.where(first, there, here)], 0)


def turn(blocks, seq_ids, token):
    tokens, width = blocks[0].shape
    rows = 4 * tokens
    wide = 2 * NARROW

    def kernel(ids_ref, own, other_chip, other_core, both, before, out_ref, place_ref, token_ref, act_ref):
        token_ref[...] = before[...]
        row = lax.axis_index("row")
        chip, core = row // 2, row % 2
        homes = [row, 2 - 2 * chip + core, 2 * chip + 1 - core, 3 - 2 * chip - core]
        for ref, home in zip((own, other_chip, other_core, both), homes):
            act_ref[pl.ds(pl.multiple_of(home * tokens, tokens), tokens), :] = ref[...]
        ids = ids_ref[...]
        for seq in range(SEQS):
            begin = jnp.sum((ids < seq).astype(jnp.int32))
            end = jnp.sum((ids <= seq).astype(jnp.int32))
            floor = begin // 16 * 16
            narrow = jnp.minimum(floor, rows - NARROW)
            is_wide = end - narrow > NARROW
            start = jnp.where(is_wide, jnp.minimum(floor, rows - wide), narrow)
            place_ref[2 * seq] = start
            place_ref[2 * seq + 1] = is_wide.astype(jnp.int32)

            def put(offset):
                here = pl.multiple_of(start + offset, 16)
                index = lax.broadcasted_iota(jnp.int32, (NARROW, width), 0) + here
                window = act_ref[pl.ds(here, NARROW), :]
                window = jnp.where((index >= begin) & (index < end), window, jnp.zeros_like(window))
                out_ref[seq, :, offset : offset + NARROW] = window.T

            put(0)
            pl.when(is_wide)(functools.partial(put, NARROW))

    return pl.pallas_call(
        kernel,
        out_shape=[
            shaped(SEQS, width, wide),
            shaped(2 * SEQS, dtype=jnp.int32),
            shaped(8, 128, dtype=F32),
        ],
        in_specs=[VMEM] * 6,
        out_specs=[VMEM, SMEM, VMEM],
        scratch_shapes=[pltpu.VMEM((rows, width), BF16)],
        compiler_params=pltpu.CompilerParams(vmem_limit_bytes=24 << 20),
    )(seq_ids.reshape(-1, 128), *blocks, token)


def correct(turned, places, blocks, known, crossed, outward):
    tokens, width = known.shape
    height, wide = turned.shape[1:]

    def kernel(place, turned, one, two, three, known, crossed, outward, out, grad, left, total, sems):
        col = lax.axis_index("col")
        inner = (col == 1) | (col == 2)

        def rows(block):
            index = jnp.where(col >= 2, 3 - block, block)
            return pl.ds(pl.multiple_of(index * tokens, tokens), tokens)

        lefts = [
            pltpu.make_async_copy(turned.at[seq], left.at[seq], sems.at[seq]) for seq in range(SEQS)
        ]
        copies = [
            pltpu.make_async_copy(ref, grad.at[rows(i + 1)], sems.at[SEQS + i])
            for i, ref in enumerate((one, two, three))
        ]
        for copy in copies + lefts:
            copy.start()
        came = jnp.where(inner, crossed[...], outward[...])
        grad[rows(0)] = (known[...] + came.astype(F32)).astype(BF16)
        for copy in copies:
            copy.wait()

        def put(columns):
            return pltpu.make_async_copy(total.at[:, columns], out.at[:, columns], sems.at[SEQS + 3])

        for seq in range(SEQS):
            lefts[seq].wait()
            start = pl.multiple_of(place[2 * seq], 16)
            is_wide = place[2 * seq + 1] == 1
            last = seq == SEQS - 1
            step = NARROW if last else width
            for begin in range(0, width, step):
                columns = slice(begin, begin + step)

                def add(depth):
                    part = dot(left[seq, :, :depth], grad[pl.ds(start, depth), columns])
                    part = part * part
                    if seq:
                        part = total[:, columns] + part
                    total[:, columns] = part / SEQS if last else part

                pl.when(is_wide)(functools.partial(add, wide))
                pl.when(jnp.logical_not(is_wide))(functools.partial(add, NARROW))
                if last:
                    put(columns).start()
        put(slice(0, width)).wait()

    return pl.pallas_call(
        kernel,
        out_shape=shaped(height, width, dtype=F32),
        in_specs=[SMEM] + [ANY] * 4 + [VMEM] * 3,
        out_specs=ANY,
        scratch_shapes=[
            pltpu.VMEM((4 * tokens, width), BF16),
            pltpu.VMEM(turned.shape, BF16),
            pltpu.VMEM((height, width), F32),
            pltpu.SemaphoreType.DMA((SEQS + 4,)),
        ],
        compiler_params=pltpu.CompilerParams(vmem_limit_bytes=24 << 20),
    )(places, turned, *blocks, known, crossed, outward)


def by_xor(values, axis, bits):
    return lax.ppermute(values, axis, [(i, i ^ bits) for i in range(4)])


def run(activations, gradients, input_basis, output_basis, seq_ids):
    depth, tokens = input_basis.shape[0], activations.shape[0]
    width = output_basis.shape[1]
    half = tokens // 2
    wide, short = shaped(tokens, width, dtype=F32), shaped(tokens, width)
    block = shaped(tokens, depth)
    parts, known, came, crossed, went = [], [None] * 4, [None] * 4, [None] * 4, [None] * 4

    def add_inward(j, token):
        def function(part, other):
            total = part[...] + other[...].astype(F32)
            return jnp.where(is_inner(), total, part[...]), total.astype(BF16)

        known[j], sent, token = step(function, [wide, short], [parts[j], came[j]], token)
        crossed[j] = lax.ppermute(sent, "col", [(1, 2), (2, 1)])
        return token

    def add_crossed(j, token):
        def function(part, other):
            return [(part[...] + other[...].astype(F32)).astype(BF16)]

        sent, token = step(function, [short], [parts[3 - j], crossed[j]], token)
        went[j] = lax.ppermute(sent, "col", [(1, 0), (2, 3)])
        return token

    def finish(j, token):
        def function(part, inner, outer):
            other = jnp.where(is_inner(), inner[...], outer[...])
            return [(part[...] + other.astype(F32)).astype(BF16)]

        return step(function, [short], [known[j], crossed[3 - j], went[3 - j]], token)

    def inward(sent):
        return lax.ppermute(sent, "col", [(0, 1), (3, 2)])

    def project_own(values, basis):
        total = dot(values[...], basis[...])
        return total, total.astype(BF16)

    def project_beside(here, there, own, basis):
        total = dot(both_halves(here[...], there[...]), basis[...])
        inner = is_inner()
        return jnp.where(inner, total, own[...]), jnp.where(inner, own[...], total), total.astype(BF16)

    def project_others(here, there, basis):
        across = both_halves(here[:half], there[:half])
        twice = both_halves(here[half:], there[half:])
        inner = is_inner()
        one = dot(jnp.where(inner, across, twice), basis[...])
        two = dot(jnp.where(inner, twice, across), basis[...])
        return one, two, one.astype(BF16), two.astype(BF16)

    def project_act(values, basis, other):
        total = dot(values[:, :depth], basis[...]) + dot(values[:, depth:], other[...])
        return total, total.astype(BF16)

    def add_there(total, other):
        return [(total[...] + other[...].astype(F32)).astype(BF16)]

    other_basis = by_xor(input_basis, "row", 1)
    beside, own, token = cut_first(gradients, depth)
    beside = by_xor(beside, "col", 1)
    own_part, sent, token = step(project_own, [wide, short], [own, output_basis], token)
    came[0] = inward(sent)
    far, mine, across, twice, token = cut_rest(activations, gradients, depth, token)
    across = by_xor(across, "col", 3)
    twice = by_xor(twice, "col", 2)
    far = by_xor(far, "row", 2)
    beside, token = step(
        lambda one: [one[...]], [shaped(half, depth)], [beside], token, after=[other_basis]
    )
    one, two, sent, token = step(
        project_beside,
        [wide, wide, short],
        [beside, by_xor(beside, "row", 1), own_part, output_basis],
        token,
    )
    parts += [one, two]
    came[1] = inward(sent)
    token = add_inward(0, token)
    pieces, token = step(
        lambda one, two: [jnp.concatenate([one[...], two[...]], 0)], [block], [across, twice], token
    )
    near_sum, sent, token = step(
        project_act, [wide, short], [mine, input_basis, other_basis], token, flops=10**11
    )
    near_there = by_xor(sent, "row", 2)
    one, two, one_sent, two_sent, token = step(
        project_others, [wide, wide, short, short], [pieces, by_xor(pieces, "row", 1), output_basis], token
    )
    parts += [one, two]
    came[2], came[3] = inward(one_sent), inward(two_sent)
    token = add_inward(1, token)
    token = add_crossed(0, token)
    far_sum, sent, token = step(project_act, [wide, short], [far, input_basis, other_basis], token)
    far_there = by_xor(sent, "row", 2)
    token = add_inward(2, token)
    token = add_crossed(1, token)
    far, token = step(add_there, [short], [far_sum, near_there], token)
    far_other = by_xor(far, "row", 1)
    token = add_inward(3, token)
    token = add_crossed(2, token)
    near, token = step(add_there, [short], [near_sum, far_there], token)
    near_other = by_xor(near, "row", 1)
    late = [None] * 4
    late[3], token = finish(3, token)
    late[2], token = finish(2, token)
    turned, places, token = turn([near, far, near_other, far_other], seq_ids, token)
    token = add_crossed(3, token)
    late[1], token = finish(1, token)
    return correct(turned, places, late[1:], known[0], crossed[3], went[3])


def on_device(rows, cols, activations, gradients, input_basis, output_basis, seq_ids):
    total = seq_ids.shape[0]
    if rows != 4 or cols != 4 or not total // 2 + 16 <= 2 * NARROW <= total:
        act_panel = project_any(activations, input_basis, "row")
        grad_panel = project_any(gradients, output_basis, "col")
        return correct_any(act_panel, grad_panel, seq_ids)
    return run(activations, gradients, input_basis, output_basis, seq_ids)


def solution(mesh):
    return jax.shard_map(
        functools.partial(on_device, mesh.shape["row"], mesh.shape["col"]),
        mesh=mesh,
        in_specs=(
            P(("grp", "row"), None),
            P(("grp", "col"), None),
            P(("grp", "row"), "col"),
            P(("grp", "col"), "row"),
            P("grp"),
        ),
        out_specs=P(("grp", "col"), "row"),
        check_vma=False,
    )
```

```python
import functools

import jax
import jax.numpy as jnp
from jax import lax
from jax.experimental import pallas as pl
from jax.experimental.pallas import tpu as pltpu
from jax.sharding import PartitionSpec as P

SEQS = 4
BF16 = jnp.bfloat16
F32 = jnp.float32
NARROW = 256
VMEM_GRANT = 24 << 20
COST = pl.CostEstimate(flops=0, bytes_accessed=0, transcendentals=0)


def dot(values, piece):
    return jnp.dot(values, piece, preferred_element_type=F32)


def outer_sum(left, right):
    return lax.dot_general(
        left, right, (((0,), (0,)), ((), ())), preferred_element_type=F32
    )


def project_any(values, basis, axis):
    turned = lax.all_to_all(values, axis, split_axis=1, concat_axis=0, tiled=True)
    total = lax.psum_scatter(dot(turned, basis), axis, scatter_dimension=0, tiled=True)
    return lax.all_gather(total.astype(BF16), axis, axis=0, tiled=True)


def correct_any(act_panel, grad_panel, seq_ids):
    total_rows = seq_ids.shape[0]
    window = total_rows // 2
    total = jnp.zeros((act_panel.shape[1], grad_panel.shape[1]), F32)
    for seq in range(SEQS):
        first = jnp.sum((seq_ids < seq).astype(jnp.int32))
        begin = jnp.minimum(first, total_rows - window)
        left = lax.dynamic_slice_in_dim(act_panel, begin, window, 0)
        right = lax.dynamic_slice_in_dim(grad_panel, begin, window, 0)
        ids_here = lax.dynamic_slice_in_dim(seq_ids, begin, window, 0)
        masked = left * (ids_here == seq).astype(BF16)[:, None]
        seq_sum = outer_sum(masked, right)
        total = total + seq_sum * seq_sum
    return total / SEQS


VMEM = pl.BlockSpec(memory_space=pltpu.VMEM)
SMEM = pl.BlockSpec(memory_space=pltpu.SMEM)
ANY = pl.BlockSpec(memory_space=pl.ANY)


def shaped(*shape, dtype=BF16):
    return jax.ShapeDtypeStruct(shape, dtype)


def columns_of(ref, rows, index, width):
    return ref.at[rows, pl.ds(pl.multiple_of(index * width, width), width)]


def copy_all(pairs, sems):
    copies = [pltpu.make_async_copy(src, dst, sems.at[i]) for i, (src, dst) in enumerate(pairs)]
    for copy in copies:
        copy.start()
    for copy in copies:
        copy.wait()


def cut_gradients(gradients, depth):
    tokens = gradients.shape[0]
    half = tokens // 2

    def kernel(grad, beside, distant, own, token, sems):
        row, col = lax.axis_index("row"), lax.axis_index("col")
        core, chip = row % 2, row // 2
        target = jnp.where(core == 0, 3 - col, col + 2 - 4 * (col // 2))

        def part(index):
            return pl.ds(pl.multiple_of(index * half, half), half)

        token[...] = jnp.zeros_like(token)
        copy_all(
            [
                (columns_of(grad, part(core), col + 1 - 2 * (col % 2), depth), beside),
                (columns_of(grad, part(chip), target, depth), distant),
                (columns_of(grad, pl.ds(0, tokens), col, depth), own),
            ],
            sems,
        )

    return pl.pallas_call(
        kernel,
        out_shape=[shaped(half, depth)] * 2 + [shaped(tokens, depth), shaped(8, 128, dtype=F32)],
        in_specs=[ANY],
        out_specs=[VMEM] * 4,
        scratch_shapes=[pltpu.SemaphoreType.DMA((3,))],
        cost_estimate=COST,
        compiler_params=pltpu.CompilerParams(vmem_limit_bytes=VMEM_GRANT),
    )(gradients)


def cut_activations(activations, depth, token):
    tokens = activations.shape[0]

    def kernel(act, before, far, mine, token, sems):
        row = lax.axis_index("row")
        core, chip = row % 2, row // 2
        whole, left, right = pl.ds(0, tokens), pl.ds(0, depth), pl.ds(depth, depth)
        token[...] = before[...]
        copy_all(
            [
                (columns_of(act, whole, 2 - 2 * chip + core, depth), far.at[:, left]),
                (columns_of(act, whole, 3 - 2 * chip - core, depth), far.at[:, right]),
                (columns_of(act, whole, 2 * chip + core, depth), mine.at[:, left]),
                (columns_of(act, whole, 2 * chip + 1 - core, depth), mine.at[:, right]),
            ],
            sems,
        )

    return pl.pallas_call(
        kernel,
        out_shape=[shaped(tokens, 2 * depth)] * 2 + [shaped(8, 128, dtype=F32)],
        in_specs=[ANY, VMEM],
        out_specs=[VMEM] * 3,
        scratch_shapes=[pltpu.SemaphoreType.DMA((4,))],
        cost_estimate=COST,
        compiler_params=pltpu.CompilerParams(vmem_limit_bytes=48 << 20),
    )(activations, token)


def step(function, shapes, values, token, after=(), grant=16 << 20):
    count, shapes = len(values), list(shapes) + [shaped(8, 128, dtype=F32)]

    def kernel(*refs):
        outs = function(*refs[:count])
        for ref, out in zip(refs[count + 1 + len(after) :], outs):
            ref[...] = out
        refs[-1][...] = refs[count][...]

    return pl.pallas_call(
        kernel,
        out_shape=shapes,
        in_specs=[VMEM] * (count + 1) + [ANY] * len(after),
        out_specs=[VMEM] * len(shapes),
        cost_estimate=COST,
        compiler_params=pltpu.CompilerParams(vmem_limit_bytes=grant),
    )(*values, token, *after)


def is_inner():
    col = lax.axis_index("col")
    return (col == 1) | (col == 2)


def both_halves(here, there, index):
    first = index == 0
    return jnp.concatenate([jnp.where(first, here, there), jnp.where(first, there, here)], 0)


def turn(blocks, seq_ids, token):
    tokens, width = blocks[0].shape
    rows = 4 * tokens
    wide = 2 * NARROW

    def kernel(ids_ref, own, other_chip, other_core, both, before, out_ref, place_ref, token_ref, act_ref):
        token_ref[...] = before[...]
        row = lax.axis_index("row")
        chip, core = row // 2, row % 2
        homes = [row, 2 - 2 * chip + core, 2 * chip + 1 - core, 3 - 2 * chip - core]
        for ref, home in zip((own, other_chip, other_core, both), homes):
            act_ref[pl.ds(pl.multiple_of(home * tokens, tokens), tokens), :] = ref[...]
        ids = ids_ref[...]
        for seq in range(SEQS):
            begin = jnp.sum((ids < seq).astype(jnp.int32))
            end = jnp.sum((ids <= seq).astype(jnp.int32))
            floor = begin // 16 * 16
            narrow = jnp.minimum(floor, rows - NARROW)
            is_wide = end - narrow > NARROW
            start = jnp.where(is_wide, jnp.minimum(floor, rows - wide), narrow)
            place_ref[2 * seq] = start
            place_ref[2 * seq + 1] = is_wide.astype(jnp.int32)

            def put(offset):
                here = pl.multiple_of(start + offset, 16)
                index = lax.broadcasted_iota(jnp.int32, (NARROW, width), 0) + here
                window = act_ref[pl.ds(here, NARROW), :]
                window = jnp.where((index >= begin) & (index < end), window, jnp.zeros_like(window))
                out_ref[seq, :, offset : offset + NARROW] = window.T

            put(0)
            pl.when(is_wide)(functools.partial(put, NARROW))

    return pl.pallas_call(
        kernel,
        out_shape=[
            shaped(SEQS, width, wide),
            shaped(2 * SEQS, dtype=jnp.int32),
            shaped(8, 128, dtype=F32),
        ],
        in_specs=[VMEM] * 6,
        out_specs=[VMEM, SMEM, VMEM],
        scratch_shapes=[pltpu.VMEM((rows, width), BF16)],
        cost_estimate=COST,
        compiler_params=pltpu.CompilerParams(vmem_limit_bytes=24 << 20),
    )(seq_ids.reshape(-1, 128), *blocks, token)


def correct(turned, places, blocks, known, crossed, outward):
    tokens, width = known.shape
    height, wide = turned.shape[1:]

    def kernel(place, turned, one, two, three, known, crossed, outward, out, grad, left, total, sems):
        col = lax.axis_index("col")
        inner = (col == 1) | (col == 2)

        def rows(block):
            index = jnp.where(col >= 2, 3 - block, block)
            return pl.ds(pl.multiple_of(index * tokens, tokens), tokens)

        lefts = [
            pltpu.make_async_copy(turned.at[seq], left.at[seq], sems.at[seq]) for seq in range(SEQS)
        ]
        copies = [
            pltpu.make_async_copy(ref, grad.at[rows(i + 1)], sems.at[SEQS + i])
            for i, ref in enumerate((one, two, three))
        ]
        for copy in copies + lefts:
            copy.start()
        came = jnp.where(inner, crossed[...], outward[...])
        grad[rows(0)] = (known[...] + came.astype(F32)).astype(BF16)
        for copy in copies:
            copy.wait()

        def put(columns):
            return pltpu.make_async_copy(total.at[:, columns], out.at[:, columns], sems.at[SEQS + 3])

        for seq in range(SEQS):
            lefts[seq].wait()
            start = pl.multiple_of(place[2 * seq], 16)
            is_wide = place[2 * seq + 1] == 1
            last = seq == SEQS - 1
            step = NARROW if last else width
            for begin in range(0, width, step):
                columns = slice(begin, begin + step)

                def add(depth):
                    part = dot(left[seq, :, :depth], grad[pl.ds(start, depth), columns])
                    part = part * part
                    if seq:
                        part = total[:, columns] + part
                    total[:, columns] = part / SEQS if last else part

                pl.when(is_wide)(functools.partial(add, wide))
                pl.when(jnp.logical_not(is_wide))(functools.partial(add, NARROW))
                if last:
                    put(columns).start()
        put(slice(0, width)).wait()

    return pl.pallas_call(
        kernel,
        out_shape=shaped(height, width, dtype=F32),
        in_specs=[SMEM] + [ANY] * 4 + [VMEM] * 3,
        out_specs=ANY,
        scratch_shapes=[
            pltpu.VMEM((4 * tokens, width), BF16),
            pltpu.VMEM(turned.shape, BF16),
            pltpu.VMEM((height, width), F32),
            pltpu.SemaphoreType.DMA((SEQS + 4,)),
        ],
        compiler_params=pltpu.CompilerParams(vmem_limit_bytes=24 << 20),
    )(places, turned, *blocks, known, crossed, outward)


def by_xor(values, axis, bits):
    return lax.ppermute(values, axis, [(i, i ^ bits) for i in range(4)])


def run(activations, gradients, input_basis, output_basis, seq_ids):
    depth, tokens = input_basis.shape[0], activations.shape[0]
    width = output_basis.shape[1]
    half = tokens // 2
    wide, short = shaped(tokens, width, dtype=F32), shaped(tokens, width)
    block, piece = shaped(tokens, depth), shaped(half, depth)
    parts, known, came, crossed, went = [], [None] * 4, [None] * 4, [None] * 4, [None] * 4

    def add_inward(j, token):
        def function(part, other):
            total = part[...] + other[...].astype(F32)
            return jnp.where(is_inner(), total, part[...]), total.astype(BF16)

        known[j], sent, token = step(function, [wide, short], [parts[j], came[j]], token)
        crossed[j] = lax.ppermute(sent, ("row", "col"), [(4 * r + c, 4 * r + 3 - c if c in (1, 2) else 4 * (r ^ 1) + c) for r in range(4) for c in range(4)])
        return token

    def add_crossed(j, token):
        def function(part, other):
            return [(part[...] + other[...].astype(F32)).astype(BF16)]

        sent, token = step(function, [short], [parts[3 - j], crossed[j]], token)
        went[j] = lax.ppermute(sent, "col", [(1, 0), (2, 3)])
        return token

    def finish(j, token):
        def function(part, inner, outer):
            other = jnp.where(is_inner(), inner[...], outer[...])
            return [(part[...] + other.astype(F32)).astype(BF16)]

        return step(function, [short], [known[j], crossed[3 - j], went[3 - j]], token)

    def inward(sent):
        return lax.ppermute(sent, "col", [(0, 1), (3, 2)])

    def project_own(values, basis):
        total = dot(values[...], basis[...])
        return total, total.astype(BF16)

    def project_beside(here, there, own, basis):
        total = dot(both_halves(here[...], there[...], lax.axis_index("row") % 2), basis[...])
        inner = is_inner()
        return jnp.where(inner, total, own[...]), jnp.where(inner, own[...], total), total.astype(BF16)

    def project_others(here, there, basis):
        straight = is_inner() == (lax.axis_index("row") % 2 == 0)
        one = dot(jnp.where(straight, here[...], there[...]), basis[...])
        two = dot(jnp.where(straight, there[...], here[...]), basis[...])
        return one, two, one.astype(BF16), two.astype(BF16)

    def project_act(values, basis, other):
        total = dot(values[:, :depth], basis[...]) + dot(values[:, depth:], other[...])
        return total, total.astype(BF16)

    def add_there(total, other):
        return [(total[...] + other[...].astype(F32)).astype(BF16)]

    other_basis = by_xor(input_basis, "row", 1)
    def same(value):
        return [value[...]]

    beside, distant, own, token = cut_gradients(gradients, depth)
    beside = by_xor(beside, "col", 1)
    distant = lax.ppermute(
        distant,
        ("row", "col"),
        [(4 * r + c, 4 * r + (c ^ 2 if r % 2 else 3 - c)) for r in range(4) for c in range(4)],
    )
    own_part, sent, token = step(project_own, [wide, short], [own, output_basis], token)
    came[0] = inward(sent)
    far, mine, token = cut_activations(activations, depth, token)
    far = by_xor(far, "row", 2)
    beside, token = step(same, [piece], [beside], token)
    distant, token = step(same, [piece], [distant], token)
    distant_there = by_xor(distant, "row", 2)
    one, two, sent, token = step(
        project_beside,
        [wide, wide, short],
        [beside, by_xor(beside, "row", 1), own_part, output_basis],
        token,
        after=[other_basis],
    )
    parts += [one, two]
    came[1] = inward(sent)
    token = add_inward(0, token)
    distant, token = step(
        lambda here, there: [both_halves(here[...], there[...], lax.axis_index("row") // 2)],
        [block],
        [distant, distant_there],
        token,
    )
    one, two, one_sent, two_sent, token = step(
        project_others,
        [wide, wide, short, short],
        [distant, by_xor(distant, "row", 1), output_basis],
        token,
    )
    parts += [one, two]
    came[2], came[3] = inward(one_sent), inward(two_sent)
    late = [None] * 4
    near_sum, sent, token = step(
        project_act, [wide, short], [mine, input_basis, other_basis], token
    )
    near_there = by_xor(sent, "row", 2)
    token = add_inward(1, token)
    token = add_crossed(0, token)
    far_sum, sent, token = step(project_act, [wide, short], [far, input_basis, other_basis], token)
    far_there = by_xor(sent, "row", 2)
    token = add_inward(2, token)
    token = add_crossed(1, token)
    far, token = step(add_there, [short], [far_sum, near_there], token)
    far_other = by_xor(far, "row", 1)
    token = add_inward(3, token)
    late[3], token = finish(3, token)
    near, token = step(add_there, [short], [near_sum, far_there], token)
    near_other = by_xor(near, "row", 1)
    token = add_crossed(2, token)
    late[2], token = finish(2, token)
    token = add_crossed(3, token)
    turned, places, token = turn([near, far, near_other, far_other], seq_ids, token)
    late[1], token = finish(1, token)
    return correct(turned, places, late[1:], known[0], crossed[3], went[3])


def on_device(rows, cols, activations, gradients, input_basis, output_basis, seq_ids):
    total = seq_ids.shape[0]
    if rows != 4 or cols != 4 or not total // 2 + 16 <= 2 * NARROW <= total:
        act_panel = project_any(activations, input_basis, "row")
        grad_panel = project_any(gradients, output_basis, "col")
        return correct_any(act_panel, grad_panel, seq_ids)
    return run(activations, gradients, input_basis, output_basis, seq_ids)


def solution(mesh):
    return jax.shard_map(
        functools.partial(on_device, mesh.shape["row"], mesh.shape["col"]),
        mesh=mesh,
        in_specs=(
            P(("grp", "row"), None),
            P(("grp", "col"), None),
            P(("grp", "row"), "col"),
            P(("grp", "col"), "row"),
            P("grp"),
        ),
        out_specs=P(("grp", "col"), "row"),
        check_vma=False,
    )
```

```python
import functools

import jax
import jax.numpy as jnp
from jax import lax
from jax.experimental import pallas as pl
from jax.experimental.pallas import tpu as pltpu
from jax.sharding import PartitionSpec as P

SEQS = 4
BF16 = jnp.bfloat16
F32 = jnp.float32
NARROW = 256
VMEM_GRANT = 24 << 20
COST = pl.CostEstimate(flops=0, bytes_accessed=0, transcendentals=0)


def dot(values, piece):
    return jnp.dot(values, piece, preferred_element_type=F32)


def outer_sum(left, right):
    return lax.dot_general(
        left, right, (((0,), (0,)), ((), ())), preferred_element_type=F32
    )


def project_any(values, basis, axis):
    turned = lax.all_to_all(values, axis, split_axis=1, concat_axis=0, tiled=True)
    total = lax.psum_scatter(dot(turned, basis), axis, scatter_dimension=0, tiled=True)
    return lax.all_gather(total.astype(BF16), axis, axis=0, tiled=True)


def correct_any(act_panel, grad_panel, seq_ids):
    total_rows = seq_ids.shape[0]
    window = total_rows // 2
    total = jnp.zeros((act_panel.shape[1], grad_panel.shape[1]), F32)
    for seq in range(SEQS):
        first = jnp.sum((seq_ids < seq).astype(jnp.int32))
        begin = jnp.minimum(first, total_rows - window)
        left = lax.dynamic_slice_in_dim(act_panel, begin, window, 0)
        right = lax.dynamic_slice_in_dim(grad_panel, begin, window, 0)
        ids_here = lax.dynamic_slice_in_dim(seq_ids, begin, window, 0)
        masked = left * (ids_here == seq).astype(BF16)[:, None]
        seq_sum = outer_sum(masked, right)
        total = total + seq_sum * seq_sum
    return total / SEQS


VMEM = pl.BlockSpec(memory_space=pltpu.VMEM)
SMEM = pl.BlockSpec(memory_space=pltpu.SMEM)
ANY = pl.BlockSpec(memory_space=pl.ANY)


def shaped(*shape, dtype=BF16):
    return jax.ShapeDtypeStruct(shape, dtype)


def columns_of(ref, rows, index, width):
    return ref.at[rows, pl.ds(pl.multiple_of(index * width, width), width)]


def copy_all(pairs, sems):
    copies = [pltpu.make_async_copy(src, dst, sems.at[i]) for i, (src, dst) in enumerate(pairs)]
    for copy in copies:
        copy.start()
    for copy in copies:
        copy.wait()


def cut_gradients(gradients, depth):
    tokens = gradients.shape[0]
    half = tokens // 2

    def kernel(grad, beside, distant, own, token, sems):
        row, col = lax.axis_index("row"), lax.axis_index("col")
        core, chip = row % 2, row // 2
        target = jnp.where(core == 0, 3 - col, col + 2 - 4 * (col // 2))

        def part(index):
            return pl.ds(pl.multiple_of(index * half, half), half)

        token[...] = jnp.zeros_like(token)
        copy_all(
            [
                (columns_of(grad, part(core), col + 1 - 2 * (col % 2), depth), beside),
                (columns_of(grad, part(chip), target, depth), distant),
                (columns_of(grad, pl.ds(0, tokens), col, depth), own),
            ],
            sems,
        )

    return pl.pallas_call(
        kernel,
        out_shape=[shaped(half, depth)] * 2 + [shaped(tokens, depth), shaped(8, 128, dtype=F32)],
        in_specs=[ANY],
        out_specs=[VMEM] * 4,
        scratch_shapes=[pltpu.SemaphoreType.DMA((3,))],
        cost_estimate=COST,
        compiler_params=pltpu.CompilerParams(vmem_limit_bytes=VMEM_GRANT),
    )(gradients)


def cut_activations(activations, depth, token):
    tokens = activations.shape[0]

    def kernel(act, before, far, mine, token, sems):
        row = lax.axis_index("row")
        core, chip = row % 2, row // 2
        whole, left, right = pl.ds(0, tokens), pl.ds(0, depth), pl.ds(depth, depth)
        token[...] = before[...]
        copy_all(
            [
                (columns_of(act, whole, 2 - 2 * chip + core, depth), far.at[:, left]),
                (columns_of(act, whole, 3 - 2 * chip - core, depth), far.at[:, right]),
                (columns_of(act, whole, 2 * chip + core, depth), mine.at[:, left]),
                (columns_of(act, whole, 2 * chip + 1 - core, depth), mine.at[:, right]),
            ],
            sems,
        )

    return pl.pallas_call(
        kernel,
        out_shape=[shaped(tokens, 2 * depth)] * 2 + [shaped(8, 128, dtype=F32)],
        in_specs=[ANY, VMEM],
        out_specs=[VMEM] * 3,
        scratch_shapes=[pltpu.SemaphoreType.DMA((4,))],
        cost_estimate=COST,
        compiler_params=pltpu.CompilerParams(vmem_limit_bytes=48 << 20),
    )(activations, token)


def step(function, shapes, values, token, after=(), grant=16 << 20):
    count, shapes = len(values), list(shapes) + [shaped(8, 128, dtype=F32)]

    def kernel(*refs):
        outs = function(*refs[:count])
        for ref, out in zip(refs[count + 1 + len(after) :], outs):
            ref[...] = out
        refs[-1][...] = refs[count][...]

    return pl.pallas_call(
        kernel,
        out_shape=shapes,
        in_specs=[VMEM] * (count + 1) + [ANY] * len(after),
        out_specs=[VMEM] * len(shapes),
        cost_estimate=COST,
        compiler_params=pltpu.CompilerParams(vmem_limit_bytes=grant),
    )(*values, token, *after)


def is_inner():
    col = lax.axis_index("col")
    return (col == 1) | (col == 2)


def both_halves(here, there, index):
    first = index == 0
    return jnp.concatenate([jnp.where(first, here, there), jnp.where(first, there, here)], 0)


def turn(blocks, seq_ids, token):
    tokens, width = blocks[0].shape
    rows = 4 * tokens
    wide = 2 * NARROW

    def kernel(ids_ref, own, other_chip, other_core, both, before, out_ref, place_ref, token_ref, act_ref):
        token_ref[...] = before[...]
        row = lax.axis_index("row")
        chip, core = row // 2, row % 2
        homes = [row, 2 - 2 * chip + core, 2 * chip + 1 - core, 3 - 2 * chip - core]
        for ref, home in zip((own, other_chip, other_core, both), homes):
            act_ref[pl.ds(pl.multiple_of(home * tokens, tokens), tokens), :] = ref[...]
        ids = ids_ref[...]
        for seq in range(SEQS):
            begin = jnp.sum((ids < seq).astype(jnp.int32))
            end = jnp.sum((ids <= seq).astype(jnp.int32))
            floor = begin // 16 * 16
            narrow = jnp.minimum(floor, rows - NARROW)
            is_wide = end - narrow > NARROW
            start = jnp.where(is_wide, jnp.minimum(floor, rows - wide), narrow)
            place_ref[2 * seq] = start
            place_ref[2 * seq + 1] = is_wide.astype(jnp.int32)

            def put(offset):
                here = pl.multiple_of(start + offset, 16)
                index = lax.broadcasted_iota(jnp.int32, (NARROW, width), 0) + here
                window = act_ref[pl.ds(here, NARROW), :]
                window = jnp.where((index >= begin) & (index < end), window, jnp.zeros_like(window))
                out_ref[seq, :, offset : offset + NARROW] = window.T

            put(0)
            pl.when(is_wide)(functools.partial(put, NARROW))

    return pl.pallas_call(
        kernel,
        out_shape=[
            shaped(SEQS, width, wide),
            shaped(2 * SEQS, dtype=jnp.int32),
            shaped(8, 128, dtype=F32),
        ],
        in_specs=[VMEM] * 6,
        out_specs=[VMEM, SMEM, VMEM],
        scratch_shapes=[pltpu.VMEM((rows, width), BF16)],
        cost_estimate=COST,
        compiler_params=pltpu.CompilerParams(vmem_limit_bytes=24 << 20),
    )(seq_ids.reshape(-1, 128), *blocks, token)


def correct(turned, places, blocks, known, crossed, outward):
    tokens, width = known.shape
    height, wide = turned.shape[1:]

    def kernel(place, turned, one, two, three, known, crossed, outward, out, grad, total, sems):
        col = lax.axis_index("col")
        inner = (col == 1) | (col == 2)

        def rows(block):
            index = jnp.where(col >= 2, 3 - block, block)
            return pl.ds(pl.multiple_of(index * tokens, tokens), tokens)

        copies = [
            pltpu.make_async_copy(ref, grad.at[rows(i + 1)], sems.at[i])
            for i, ref in enumerate((one, two, three))
        ]
        for copy in copies:
            copy.start()
        came = jnp.where(inner, crossed[...], outward[...])
        grad[rows(0)] = (known[...] + came.astype(F32)).astype(BF16)
        for copy in copies:
            copy.wait()

        def put(columns):
            return pltpu.make_async_copy(total.at[:, columns], out.at[:, columns], sems.at[3])

        for seq in range(SEQS):
            start = pl.multiple_of(place[2 * seq], 16)
            is_wide = place[2 * seq + 1] == 1
            last = seq == SEQS - 1
            step = NARROW if last else width
            for begin in range(0, width, step):
                columns = slice(begin, begin + step)

                def add(depth):
                    part = dot(turned[seq, :, :depth], grad[pl.ds(start, depth), columns])
                    part = part * part
                    if seq:
                        part = total[:, columns] + part
                    total[:, columns] = part / SEQS if last else part

                pl.when(is_wide)(functools.partial(add, wide))
                pl.when(jnp.logical_not(is_wide))(functools.partial(add, NARROW))
                if last:
                    put(columns).start()
        put(slice(0, width)).wait()

    return pl.pallas_call(
        kernel,
        out_shape=shaped(height, width, dtype=F32),
        in_specs=[SMEM, VMEM] + [ANY] * 3 + [VMEM] * 3,
        out_specs=ANY,
        scratch_shapes=[
            pltpu.VMEM((4 * tokens, width), BF16),
            pltpu.VMEM((height, width), F32),
            pltpu.SemaphoreType.DMA((4,)),
        ],
        compiler_params=pltpu.CompilerParams(vmem_limit_bytes=24 << 20),
    )(places, turned, *blocks, known, crossed, outward)


def by_xor(values, axis, bits):
    return lax.ppermute(values, axis, [(i, i ^ bits) for i in range(4)])


def run(activations, gradients, input_basis, output_basis, seq_ids):
    depth, tokens = input_basis.shape[0], activations.shape[0]
    width = output_basis.shape[1]
    half = tokens // 2
    wide, short = shaped(tokens, width, dtype=F32), shaped(tokens, width)
    block, piece = shaped(tokens, depth), shaped(half, depth)
    parts, known, came, crossed, went = [], [None] * 4, [None] * 4, [None] * 4, [None] * 4

    def add_inward(j, token):
        def function(part, other):
            total = part[...] + other[...].astype(F32)
            return jnp.where(is_inner(), total, part[...]), total.astype(BF16)

        known[j], sent, token = step(function, [wide, short], [parts[j], came[j]], token)
        crossed[j] = lax.ppermute(sent, ("row", "col"), [(4 * r + c, 4 * r + 3 - c if c in (1, 2) else 4 * (r ^ 1) + c) for r in range(4) for c in range(4)])
        return token

    def add_crossed(j, token):
        def function(part, other):
            return [(part[...] + other[...].astype(F32)).astype(BF16)]

        sent, token = step(function, [short], [parts[3 - j], crossed[j]], token)
        went[j] = lax.ppermute(sent, "col", [(1, 0), (2, 3)])
        return token

    def finish(j, token):
        def function(part, inner, outer):
            other = jnp.where(is_inner(), inner[...], outer[...])
            return [(part[...] + other.astype(F32)).astype(BF16)]

        return step(function, [short], [known[j], crossed[3 - j], went[3 - j]], token)

    def inward(sent):
        return lax.ppermute(sent, "col", [(0, 1), (3, 2)])

    def project_own(values, basis):
        total = dot(values[...], basis[...])
        return total, total.astype(BF16)

    def project_beside(here, there, own, basis):
        total = dot(both_halves(here[...], there[...], lax.axis_index("row") % 2), basis[...])
        inner = is_inner()
        return jnp.where(inner, total, own[...]), jnp.where(inner, own[...], total), total.astype(BF16)

    def project_others(here, there, basis):
        straight = is_inner() == (lax.axis_index("row") % 2 == 0)
        one = dot(jnp.where(straight, here[...], there[...]), basis[...])
        two = dot(jnp.where(straight, there[...], here[...]), basis[...])
        return one, two, one.astype(BF16), two.astype(BF16)

    def project_act(values, basis, other):
        total = dot(values[:, :depth], basis[...]) + dot(values[:, depth:], other[...])
        return total, total.astype(BF16)

    def add_there(total, other):
        return [(total[...] + other[...].astype(F32)).astype(BF16)]

    other_basis = by_xor(input_basis, "row", 1)
    def same(value):
        return [value[...]]

    beside, distant, own, token = cut_gradients(gradients, depth)
    beside = by_xor(beside, "col", 1)
    distant = lax.ppermute(
        distant,
        ("row", "col"),
        [(4 * r + c, 4 * r + (c ^ 2 if r % 2 else 3 - c)) for r in range(4) for c in range(4)],
    )
    own_part, sent, token = step(project_own, [wide, short], [own, output_basis], token)
    came[0] = inward(sent)
    far, mine, token = cut_activations(activations, depth, token)
    far = by_xor(far, "row", 2)
    beside, token = step(same, [piece], [beside], token)
    distant, token = step(same, [piece], [distant], token)
    distant_there = by_xor(distant, "row", 2)
    one, two, sent, token = step(
        project_beside,
        [wide, wide, short],
        [beside, by_xor(beside, "row", 1), own_part, output_basis],
        token,
        after=[other_basis],
    )
    parts += [one, two]
    came[1] = inward(sent)
    token = add_inward(0, token)
    distant, token = step(
        lambda here, there: [both_halves(here[...], there[...], lax.axis_index("row") // 2)],
        [block],
        [distant, distant_there],
        token,
    )
    one, two, one_sent, two_sent, token = step(
        project_others,
        [wide, wide, short, short],
        [distant, by_xor(distant, "row", 1), output_basis],
        token,
    )
    parts += [one, two]
    came[2], came[3] = inward(one_sent), inward(two_sent)
    late = [None] * 4
    near_sum, sent, token = step(
        project_act, [wide, short], [mine, input_basis, other_basis], token
    )
    near_there = by_xor(sent, "row", 2)
    token = add_inward(1, token)
    token = add_crossed(0, token)
    far_sum, sent, token = step(project_act, [wide, short], [far, input_basis, other_basis], token)
    far_there = by_xor(sent, "row", 2)
    token = add_inward(2, token)
    token = add_crossed(1, token)
    far, token = step(add_there, [short], [far_sum, near_there], token)
    far_other = by_xor(far, "row", 1)
    token = add_inward(3, token)
    late[3], token = finish(3, token)
    token = add_crossed(2, token)
    near, token = step(add_there, [short], [near_sum, far_there], token)
    near_other = by_xor(near, "row", 1)
    late[2], token = finish(2, token)
    token = add_crossed(3, token)
    turned, places, token = turn([near, far, near_other, far_other], seq_ids, token)
    late[1], token = finish(1, token)
    return correct(turned, places, late[1:], known[0], crossed[3], went[3])


def on_device(rows, cols, activations, gradients, input_basis, output_basis, seq_ids):
    total = seq_ids.shape[0]
    if rows != 4 or cols != 4 or not total // 2 + 16 <= 2 * NARROW <= total:
        act_panel = project_any(activations, input_basis, "row")
        grad_panel = project_any(gradients, output_basis, "col")
        return correct_any(act_panel, grad_panel, seq_ids)
    return run(activations, gradients, input_basis, output_basis, seq_ids)


def solution(mesh):
    return jax.shard_map(
        functools.partial(on_device, mesh.shape["row"], mesh.shape["col"]),
        mesh=mesh,
        in_specs=(
            P(("grp", "row"), None),
            P(("grp", "col"), None),
            P(("grp", "row"), "col"),
            P(("grp", "col"), "row"),
            P("grp"),
        ),
        out_specs=P(("grp", "col"), "row"),
        check_vma=False,
    )
```

```python
import functools

import jax
import jax.numpy as jnp
from jax import lax
from jax.experimental import pallas as pl
from jax.experimental.pallas import tpu as pltpu
from jax.sharding import PartitionSpec as P

SEQS = 4
BF16 = jnp.bfloat16
F32 = jnp.float32
NARROW = 256
VMEM_GRANT = 24 << 20
COST = pl.CostEstimate(flops=0, bytes_accessed=0, transcendentals=0)


def dot(values, piece):
    return jnp.dot(values, piece, preferred_element_type=F32)


def outer_sum(left, right):
    return lax.dot_general(
        left, right, (((0,), (0,)), ((), ())), preferred_element_type=F32
    )


def project_any(values, basis, axis):
    turned = lax.all_to_all(values, axis, split_axis=1, concat_axis=0, tiled=True)
    total = lax.psum_scatter(dot(turned, basis), axis, scatter_dimension=0, tiled=True)
    return lax.all_gather(total.astype(BF16), axis, axis=0, tiled=True)


def correct_any(act_panel, grad_panel, seq_ids):
    total_rows = seq_ids.shape[0]
    window = total_rows // 2
    total = jnp.zeros((act_panel.shape[1], grad_panel.shape[1]), F32)
    for seq in range(SEQS):
        first = jnp.sum((seq_ids < seq).astype(jnp.int32))
        begin = jnp.minimum(first, total_rows - window)
        left = lax.dynamic_slice_in_dim(act_panel, begin, window, 0)
        right = lax.dynamic_slice_in_dim(grad_panel, begin, window, 0)
        ids_here = lax.dynamic_slice_in_dim(seq_ids, begin, window, 0)
        masked = left * (ids_here == seq).astype(BF16)[:, None]
        seq_sum = outer_sum(masked, right)
        total = total + seq_sum * seq_sum
    return total / SEQS


VMEM = pl.BlockSpec(memory_space=pltpu.VMEM)
SMEM = pl.BlockSpec(memory_space=pltpu.SMEM)
ANY = pl.BlockSpec(memory_space=pl.ANY)


def shaped(*shape, dtype=BF16):
    return jax.ShapeDtypeStruct(shape, dtype)


def columns_of(ref, rows, index, width):
    return ref.at[rows, pl.ds(pl.multiple_of(index * width, width), width)]


def copy_all(pairs, sems):
    copies = [pltpu.make_async_copy(src, dst, sems.at[i]) for i, (src, dst) in enumerate(pairs)]
    for copy in copies:
        copy.start()
    for copy in copies:
        copy.wait()


def cut_gradients(gradients, depth):
    tokens = gradients.shape[0]
    half = tokens // 2

    def kernel(grad, beside, distant, own, token, sems):
        row, col = lax.axis_index("row"), lax.axis_index("col")
        core, chip = row % 2, row // 2
        target = jnp.where(core == 0, 3 - col, col + 2 - 4 * (col // 2))

        def part(index):
            return pl.ds(pl.multiple_of(index * half, half), half)

        token[...] = jnp.zeros_like(token)
        copy_all(
            [
                (columns_of(grad, part(core), col + 1 - 2 * (col % 2), depth), beside),
                (columns_of(grad, part(chip), target, depth), distant),
                (columns_of(grad, pl.ds(0, tokens), col, depth), own),
            ],
            sems,
        )

    return pl.pallas_call(
        kernel,
        out_shape=[shaped(half, depth)] * 2 + [shaped(tokens, depth), shaped(8, 128, dtype=F32)],
        in_specs=[ANY],
        out_specs=[VMEM] * 4,
        scratch_shapes=[pltpu.SemaphoreType.DMA((3,))],
        cost_estimate=COST,
        compiler_params=pltpu.CompilerParams(vmem_limit_bytes=VMEM_GRANT),
    )(gradients)


def cut_activations(activations, depth, token):
    tokens = activations.shape[0]

    def kernel(act, before, far, mine, token, sems):
        row = lax.axis_index("row")
        core, chip = row % 2, row // 2
        whole, left, right = pl.ds(0, tokens), pl.ds(0, depth), pl.ds(depth, depth)
        token[...] = before[...]
        copy_all(
            [
                (columns_of(act, whole, 2 - 2 * chip + core, depth), far.at[:, left]),
                (columns_of(act, whole, 3 - 2 * chip - core, depth), far.at[:, right]),
                (columns_of(act, whole, 2 * chip + core, depth), mine.at[:, left]),
                (columns_of(act, whole, 2 * chip + 1 - core, depth), mine.at[:, right]),
            ],
            sems,
        )

    return pl.pallas_call(
        kernel,
        out_shape=[shaped(tokens, 2 * depth)] * 2 + [shaped(8, 128, dtype=F32)],
        in_specs=[ANY, VMEM],
        out_specs=[VMEM] * 3,
        scratch_shapes=[pltpu.SemaphoreType.DMA((4,))],
        cost_estimate=COST,
        compiler_params=pltpu.CompilerParams(vmem_limit_bytes=48 << 20),
    )(activations, token)


def step(function, shapes, values, token, after=(), grant=16 << 20):
    count, shapes = len(values), list(shapes) + [shaped(8, 128, dtype=F32)]

    def kernel(*refs):
        outs = function(*refs[:count])
        for ref, out in zip(refs[count + 1 + len(after) :], outs):
            ref[...] = out
        refs[-1][...] = refs[count][...]

    return pl.pallas_call(
        kernel,
        out_shape=shapes,
        in_specs=[VMEM] * (count + 1) + [ANY] * len(after),
        out_specs=[VMEM] * len(shapes),
        cost_estimate=COST,
        compiler_params=pltpu.CompilerParams(vmem_limit_bytes=grant),
    )(*values, token, *after)


def is_inner():
    col = lax.axis_index("col")
    return (col == 1) | (col == 2)


def both_halves(here, there, index):
    first = index == 0
    return jnp.concatenate([jnp.where(first, here, there), jnp.where(first, there, here)], 0)


def turn(blocks, seq_ids, token):
    tokens, width = blocks[0].shape
    rows = 4 * tokens
    wide = 2 * NARROW

    def kernel(ids_ref, own, other_chip, other_core, both, before, out_ref, place_ref, token_ref, act_ref):
        token_ref[...] = before[...]
        row = lax.axis_index("row")
        chip, core = row // 2, row % 2
        homes = [row, 2 - 2 * chip + core, 2 * chip + 1 - core, 3 - 2 * chip - core]
        for ref, home in zip((own, other_chip, other_core, both), homes):
            act_ref[pl.ds(pl.multiple_of(home * tokens, tokens), tokens), :] = ref[...]
        ids = ids_ref[...]
        for seq in range(SEQS):
            begin = jnp.sum((ids < seq).astype(jnp.int32))
            end = jnp.sum((ids <= seq).astype(jnp.int32))
            floor = begin // 16 * 16
            narrow = jnp.minimum(floor, rows - NARROW)
            is_wide = end - narrow > NARROW
            start = jnp.where(is_wide, jnp.minimum(floor, rows - wide), narrow)
            place_ref[2 * seq] = start
            place_ref[2 * seq + 1] = is_wide.astype(jnp.int32)

            def put(offset):
                here = pl.multiple_of(start + offset, 16)
                index = lax.broadcasted_iota(jnp.int32, (NARROW, width), 0) + here
                window = act_ref[pl.ds(here, NARROW), :]
                window = jnp.where((index >= begin) & (index < end), window, jnp.zeros_like(window))
                out_ref[seq, :, offset : offset + NARROW] = window.T

            put(0)
            pl.when(is_wide)(functools.partial(put, NARROW))

    return pl.pallas_call(
        kernel,
        out_shape=[
            shaped(SEQS, width, wide),
            shaped(2 * SEQS, dtype=jnp.int32),
            shaped(8, 128, dtype=F32),
        ],
        in_specs=[VMEM] * 6,
        out_specs=[VMEM, SMEM, VMEM],
        scratch_shapes=[pltpu.VMEM((rows, width), BF16)],
        cost_estimate=COST,
        compiler_params=pltpu.CompilerParams(vmem_limit_bytes=24 << 20),
    )(seq_ids.reshape(-1, 128), *blocks, token)


def correct(turned, places, blocks, known, crossed, outward):
    tokens, width = known.shape
    height, wide = turned.shape[1:]

    def kernel(place, turned, one, two, three, known, crossed, outward, out, grad, total, sems):
        col = lax.axis_index("col")
        inner = (col == 1) | (col == 2)

        def rows(block):
            index = jnp.where(col >= 2, 3 - block, block)
            return pl.ds(pl.multiple_of(index * tokens, tokens), tokens)

        copies = [
            pltpu.make_async_copy(ref, grad.at[rows(i + 1)], sems.at[i])
            for i, ref in enumerate((one, two, three))
        ]
        for copy in copies:
            copy.start()
        came = jnp.where(inner, crossed[...], outward[...])
        grad[rows(0)] = (known[...] + came.astype(F32)).astype(BF16)
        for copy in copies:
            copy.wait()

        def put(columns):
            return pltpu.make_async_copy(total.at[:, columns], out.at[:, columns], sems.at[3])

        for seq in range(SEQS):
            start = pl.multiple_of(place[2 * seq], 16)
            is_wide = place[2 * seq + 1] == 1
            last = seq == SEQS - 1
            step = NARROW if last else width
            for begin in range(0, width, step):
                columns = slice(begin, begin + step)

                def add(depth):
                    part = dot(turned[seq, :, :depth], grad[pl.ds(start, depth), columns])
                    part = part * part
                    if seq:
                        part = total[:, columns] + part
                    total[:, columns] = part / SEQS if last else part

                pl.when(is_wide)(functools.partial(add, wide))
                pl.when(jnp.logical_not(is_wide))(functools.partial(add, NARROW))
                if last:
                    put(columns).start()
        put(slice(0, width)).wait()

    return pl.pallas_call(
        kernel,
        out_shape=shaped(height, width, dtype=F32),
        in_specs=[SMEM, VMEM] + [ANY] * 3 + [VMEM] * 3,
        out_specs=ANY,
        scratch_shapes=[
            pltpu.VMEM((4 * tokens, width), BF16),
            pltpu.VMEM((height, width), F32),
            pltpu.SemaphoreType.DMA((4,)),
        ],
        compiler_params=pltpu.CompilerParams(vmem_limit_bytes=24 << 20),
    )(places, turned, *blocks, known, crossed, outward)


def by_xor(values, axis, bits):
    return lax.ppermute(values, axis, [(i, i ^ bits) for i in range(4)])


def run(activations, gradients, input_basis, output_basis, seq_ids):
    depth, tokens = input_basis.shape[0], activations.shape[0]
    width = output_basis.shape[1]
    half = tokens // 2
    wide, short = shaped(tokens, width, dtype=F32), shaped(tokens, width)
    block, piece = shaped(tokens, depth), shaped(half, depth)
    parts, known, came, crossed, went = [], [None] * 4, [None] * 4, [None] * 4, [None] * 4

    def add_inward(j, token):
        def function(part, other):
            total = part[...] + other[...].astype(F32)
            return jnp.where(is_inner(), total, part[...]), total.astype(BF16)

        known[j], sent, token = step(function, [wide, short], [parts[j], came[j]], token)
        crossed[j] = lax.ppermute(sent, ("row", "col"), [(4 * r + c, 4 * r + 3 - c if c in (1, 2) else 4 * (r ^ 1) + c) for r in range(4) for c in range(4)])
        return token

    def add_crossed(j, token):
        def function(part, other):
            return [(part[...] + other[...].astype(F32)).astype(BF16)]

        sent, token = step(function, [short], [parts[3 - j], crossed[j]], token)
        went[j] = lax.ppermute(sent, "col", [(1, 0), (2, 3)])
        return token

    def finish(j, token):
        def function(part, inner, outer):
            other = jnp.where(is_inner(), inner[...], outer[...])
            return [(part[...] + other.astype(F32)).astype(BF16)]

        return step(function, [short], [known[j], crossed[3 - j], went[3 - j]], token)

    def inward(sent):
        return lax.ppermute(sent, "col", [(0, 1), (3, 2)])

    def project_own(values, basis):
        total = dot(values[...], basis[...])
        return total, total.astype(BF16)

    def project_beside(here, there, own, basis):
        total = dot(both_halves(here[...], there[...], lax.axis_index("row") % 2), basis[...])
        inner = is_inner()
        return jnp.where(inner, total, own[...]), jnp.where(inner, own[...], total), total.astype(BF16)

    def project_others(here, there, basis):
        straight = is_inner() == (lax.axis_index("row") % 2 == 0)
        one = dot(jnp.where(straight, here[...], there[...]), basis[...])
        two = dot(jnp.where(straight, there[...], here[...]), basis[...])
        return one, two, one.astype(BF16), two.astype(BF16)

    def project_act(values, basis, other):
        total = dot(values[:, :depth], basis[...]) + dot(values[:, depth:], other[...])
        return total, total.astype(BF16)

    def add_there(total, other):
        return [(total[...] + other[...].astype(F32)).astype(BF16)]

    other_basis = by_xor(input_basis, "row", 1)
    def same(value):
        return [value[...]]

    beside, distant, own, token = cut_gradients(gradients, depth)
    beside = by_xor(beside, "col", 1)
    distant = lax.ppermute(
        distant,
        ("row", "col"),
        [(4 * r + c, 4 * r + (c ^ 2 if r % 2 else 3 - c)) for r in range(4) for c in range(4)],
    )
    own_part, sent, token = step(project_own, [wide, short], [own, output_basis], token)
    came[0] = inward(sent)
    far, mine, token = cut_activations(activations, depth, token)
    far = by_xor(far, "row", 2)
    beside, token = step(same, [piece], [beside], token)
    distant, token = step(same, [piece], [distant], token)
    distant_there = by_xor(distant, "row", 2)
    one, two, sent, token = step(
        project_beside,
        [wide, wide, short],
        [beside, by_xor(beside, "row", 1), own_part, output_basis],
        token,
        after=[other_basis],
    )
    parts += [one, two]
    came[1] = inward(sent)
    token = add_inward(0, token)
    distant, token = step(
        lambda here, there: [both_halves(here[...], there[...], lax.axis_index("row") // 2)],
        [block],
        [distant, distant_there],
        token,
    )
    one, two, one_sent, two_sent, token = step(
        project_others,
        [wide, wide, short, short],
        [distant, by_xor(distant, "row", 1), output_basis],
        token,
    )
    parts += [one, two]
    came[2], came[3] = inward(one_sent), inward(two_sent)
    late = [None] * 4
    near_sum, sent, token = step(
        project_act, [wide, short], [mine, input_basis, other_basis], token
    )
    near_there = by_xor(sent, "row", 2)
    token = add_inward(1, token)
    token = add_crossed(0, token)
    far_sum, sent, token = step(project_act, [wide, short], [far, input_basis, other_basis], token)
    far_there = by_xor(sent, "row", 2)
    token = add_inward(2, token)
    token = add_crossed(1, token)
    far, token = step(add_there, [short], [far_sum, near_there], token)
    far_other = by_xor(far, "row", 1)
    token = add_inward(3, token)
    late[3], token = finish(3, token)
    near, token = step(add_there, [short], [near_sum, far_there], token)
    near_other = by_xor(near, "row", 1)
    token = add_crossed(2, token)
    late[2], token = finish(2, token)
    token = add_crossed(3, token)
    late[1], token = finish(1, token)
    turned, places, token = turn([near, far, near_other, far_other], seq_ids, token)
    return correct(turned, places, late[1:], known[0], crossed[3], went[3])


def on_device(rows, cols, activations, gradients, input_basis, output_basis, seq_ids):
    total = seq_ids.shape[0]
    if rows != 4 or cols != 4 or not total // 2 + 16 <= 2 * NARROW <= total:
        act_panel = project_any(activations, input_basis, "row")
        grad_panel = project_any(gradients, output_basis, "col")
        return correct_any(act_panel, grad_panel, seq_ids)
    return run(activations, gradients, input_basis, output_basis, seq_ids)


def solution(mesh):
    return jax.shard_map(
        functools.partial(on_device, mesh.shape["row"], mesh.shape["col"]),
        mesh=mesh,
        in_specs=(
            P(("grp", "row"), None),
            P(("grp", "col"), None),
            P(("grp", "row"), "col"),
            P(("grp", "col"), "row"),
            P("grp"),
        ),
        out_specs=P(("grp", "col"), "row"),
        check_vma=False,
    )
```

```python
import functools

import jax
import jax.numpy as jnp
from jax import lax
from jax.experimental import pallas as pl
from jax.experimental.pallas import tpu as pltpu
from jax.sharding import PartitionSpec as P

SEQS = 4
BF16 = jnp.bfloat16
F32 = jnp.float32
NARROW = 256
VMEM_GRANT = 24 << 20
COST = pl.CostEstimate(flops=0, bytes_accessed=0, transcendentals=0)


def dot(values, piece):
    return jnp.dot(values, piece, preferred_element_type=F32)


def outer_sum(left, right):
    return lax.dot_general(
        left, right, (((0,), (0,)), ((), ())), preferred_element_type=F32
    )


def project_any(values, basis, axis):
    turned = lax.all_to_all(values, axis, split_axis=1, concat_axis=0, tiled=True)
    total = lax.psum_scatter(dot(turned, basis), axis, scatter_dimension=0, tiled=True)
    return lax.all_gather(total.astype(BF16), axis, axis=0, tiled=True)


def correct_any(act_panel, grad_panel, seq_ids):
    total_rows = seq_ids.shape[0]
    window = total_rows // 2
    total = jnp.zeros((act_panel.shape[1], grad_panel.shape[1]), F32)
    for seq in range(SEQS):
        first = jnp.sum((seq_ids < seq).astype(jnp.int32))
        begin = jnp.minimum(first, total_rows - window)
        left = lax.dynamic_slice_in_dim(act_panel, begin, window, 0)
        right = lax.dynamic_slice_in_dim(grad_panel, begin, window, 0)
        ids_here = lax.dynamic_slice_in_dim(seq_ids, begin, window, 0)
        masked = left * (ids_here == seq).astype(BF16)[:, None]
        seq_sum = outer_sum(masked, right)
        total = total + seq_sum * seq_sum
    return total / SEQS


VMEM = pl.BlockSpec(memory_space=pltpu.VMEM)
SMEM = pl.BlockSpec(memory_space=pltpu.SMEM)
ANY = pl.BlockSpec(memory_space=pl.ANY)


def shaped(*shape, dtype=BF16):
    return jax.ShapeDtypeStruct(shape, dtype)


def columns_of(ref, rows, index, width):
    return ref.at[rows, pl.ds(pl.multiple_of(index * width, width), width)]


def copy_all(pairs, sems):
    copies = [pltpu.make_async_copy(src, dst, sems.at[i]) for i, (src, dst) in enumerate(pairs)]
    for copy in copies:
        copy.start()
    for copy in copies:
        copy.wait()


def cut_gradients(gradients, depth):
    tokens = gradients.shape[0]
    half = tokens // 2

    def kernel(grad, beside, distant, own, token, sems):
        row, col = lax.axis_index("row"), lax.axis_index("col")
        core, chip = row % 2, row // 2
        target = jnp.where(core == 0, 3 - col, col + 2 - 4 * (col // 2))

        def part(index):
            return pl.ds(pl.multiple_of(index * half, half), half)

        token[...] = jnp.zeros_like(token)
        copy_all(
            [
                (columns_of(grad, part(core), col + 1 - 2 * (col % 2), depth), beside),
                (columns_of(grad, part(chip), target, depth), distant),
                (columns_of(grad, pl.ds(0, tokens), col, depth), own),
            ],
            sems,
        )

    return pl.pallas_call(
        kernel,
        out_shape=[shaped(half, depth)] * 2 + [shaped(tokens, depth), shaped(8, 128, dtype=F32)],
        in_specs=[ANY],
        out_specs=[VMEM] * 4,
        scratch_shapes=[pltpu.SemaphoreType.DMA((3,))],
        cost_estimate=COST,
        compiler_params=pltpu.CompilerParams(vmem_limit_bytes=VMEM_GRANT),
    )(gradients)


def cut_activations(activations, depth, token):
    tokens = activations.shape[0]

    def kernel(act, before, far, mine, token, sems):
        row = lax.axis_index("row")
        core, chip = row % 2, row // 2
        whole, left, right = pl.ds(0, tokens), pl.ds(0, depth), pl.ds(depth, depth)
        token[...] = before[...]
        copy_all(
            [
                (columns_of(act, whole, 2 - 2 * chip + core, depth), far.at[:, left]),
                (columns_of(act, whole, 3 - 2 * chip - core, depth), far.at[:, right]),
                (columns_of(act, whole, 2 * chip + core, depth), mine.at[:, left]),
                (columns_of(act, whole, 2 * chip + 1 - core, depth), mine.at[:, right]),
            ],
            sems,
        )

    return pl.pallas_call(
        kernel,
        out_shape=[shaped(tokens, 2 * depth)] * 2 + [shaped(8, 128, dtype=F32)],
        in_specs=[ANY, VMEM],
        out_specs=[VMEM] * 3,
        scratch_shapes=[pltpu.SemaphoreType.DMA((4,))],
        cost_estimate=COST,
        compiler_params=pltpu.CompilerParams(vmem_limit_bytes=48 << 20),
    )(activations, token)


def step(function, shapes, values, token, after=(), grant=16 << 20):
    count, shapes = len(values), list(shapes) + [shaped(8, 128, dtype=F32)]

    def kernel(*refs):
        outs = function(*refs[:count])
        for ref, out in zip(refs[count + 1 + len(after) :], outs):
            ref[...] = out
        refs[-1][...] = refs[count][...]

    return pl.pallas_call(
        kernel,
        out_shape=shapes,
        in_specs=[VMEM] * (count + 1) + [ANY] * len(after),
        out_specs=[VMEM] * len(shapes),
        cost_estimate=COST,
        compiler_params=pltpu.CompilerParams(vmem_limit_bytes=grant),
    )(*values, token, *after)


def is_inner():
    col = lax.axis_index("col")
    return (col == 1) | (col == 2)


def both_halves(here, there, index):
    first = index == 0
    return jnp.concatenate([jnp.where(first, here, there), jnp.where(first, there, here)], 0)


def turn(blocks, seq_ids, token):
    tokens, width = blocks[0].shape
    rows = 4 * tokens
    wide = 2 * NARROW

    def kernel(ids_ref, own, other_chip, other_core, both, before, out_ref, place_ref, token_ref, act_ref):
        token_ref[...] = before[...]
        row = lax.axis_index("row")
        chip, core = row // 2, row % 2
        homes = [row, 2 - 2 * chip + core, 2 * chip + 1 - core, 3 - 2 * chip - core]
        for ref, home in zip((own, other_chip, other_core, both), homes):
            act_ref[pl.ds(pl.multiple_of(home * tokens, tokens), tokens), :] = ref[...]
        ids = ids_ref[...]
        for seq in range(SEQS):
            begin = jnp.sum((ids < seq).astype(jnp.int32))
            end = jnp.sum((ids <= seq).astype(jnp.int32))
            floor = begin // 16 * 16
            narrow = jnp.minimum(floor, rows - NARROW)
            is_wide = end - narrow > NARROW
            start = jnp.where(is_wide, jnp.minimum(floor, rows - wide), narrow)
            place_ref[2 * seq] = start
            place_ref[2 * seq + 1] = is_wide.astype(jnp.int32)

            def put(offset):
                here = pl.multiple_of(start + offset, 16)
                index = lax.broadcasted_iota(jnp.int32, (NARROW, width), 0) + here
                window = act_ref[pl.ds(here, NARROW), :]
                window = jnp.where((index >= begin) & (index < end), window, jnp.zeros_like(window))
                out_ref[seq, :, offset : offset + NARROW] = window.T

            put(0)
            pl.when(is_wide)(functools.partial(put, NARROW))

    return pl.pallas_call(
        kernel,
        out_shape=[
            shaped(SEQS, width, wide),
            shaped(2 * SEQS, dtype=jnp.int32),
            shaped(8, 128, dtype=F32),
        ],
        in_specs=[VMEM] * 6,
        out_specs=[VMEM, SMEM, VMEM],
        scratch_shapes=[pltpu.VMEM((rows, width), BF16)],
        cost_estimate=COST,
        compiler_params=pltpu.CompilerParams(vmem_limit_bytes=24 << 20),
    )(seq_ids.reshape(-1, 128), *blocks, token)


def correct(turned, places, blocks, known, crossed, outward):
    tokens, width = known.shape
    height, wide = turned.shape[1:]

    def kernel(place, turned, one, two, three, known, crossed, outward, out, grad, total, sems):
        col = lax.axis_index("col")
        inner = (col == 1) | (col == 2)

        def rows(block):
            index = jnp.where(col >= 2, 3 - block, block)
            return pl.ds(pl.multiple_of(index * tokens, tokens), tokens)

        copies = [
            pltpu.make_async_copy(ref, grad.at[rows(i + 1)], sems.at[i])
            for i, ref in enumerate((one, two, three))
        ]
        for copy in copies:
            copy.start()
        came = jnp.where(inner, crossed[...], outward[...])
        grad[rows(0)] = (known[...] + came.astype(F32)).astype(BF16)
        for copy in copies:
            copy.wait()

        def put(columns):
            return pltpu.make_async_copy(total.at[:, columns], out.at[:, columns], sems.at[3])

        def add_sequence(seq, columns):
            start = pl.multiple_of(place[2 * seq], 16)
            is_wide = place[2 * seq + 1] == 1

            def add(depth):
                part = dot(turned[seq, :, :depth], grad[pl.ds(start, depth), columns])
                part = part * part
                if seq:
                    part = total[:, columns] + part
                total[:, columns] = part / SEQS if seq == SEQS - 1 else part

            pl.when(is_wide)(functools.partial(add, wide))
            pl.when(jnp.logical_not(is_wide))(functools.partial(add, NARROW))

        for seq in range(SEQS - 2):
            add_sequence(seq, slice(0, width))
        for begin in range(0, width, NARROW):
            columns = slice(begin, begin + NARROW)
            for seq in (SEQS - 2, SEQS - 1):
                add_sequence(seq, columns)
            put(columns).start()
        put(slice(0, width)).wait()

    return pl.pallas_call(
        kernel,
        out_shape=shaped(height, width, dtype=F32),
        in_specs=[SMEM, VMEM] + [ANY] * 3 + [VMEM] * 3,
        out_specs=ANY,
        scratch_shapes=[
            pltpu.VMEM((4 * tokens, width), BF16),
            pltpu.VMEM((height, width), F32),
            pltpu.SemaphoreType.DMA((4,)),
        ],
        compiler_params=pltpu.CompilerParams(vmem_limit_bytes=24 << 20),
    )(places, turned, *blocks, known, crossed, outward)


def by_xor(values, axis, bits):
    return lax.ppermute(values, axis, [(i, i ^ bits) for i in range(4)])


def run(activations, gradients, input_basis, output_basis, seq_ids):
    depth, tokens = input_basis.shape[0], activations.shape[0]
    width = output_basis.shape[1]
    half = tokens // 2
    wide, short = shaped(tokens, width, dtype=F32), shaped(tokens, width)
    block, piece = shaped(tokens, depth), shaped(half, depth)
    parts, known, came, crossed, went = [], [None] * 4, [None] * 4, [None] * 4, [None] * 4

    def add_inward(j, token):
        def function(part, other):
            total = part[...] + other[...].astype(F32)
            return jnp.where(is_inner(), total, part[...]), total.astype(BF16)

        known[j], sent, token = step(function, [wide, short], [parts[j], came[j]], token)
        crossed[j] = lax.ppermute(sent, ("row", "col"), [(4 * r + c, 4 * r + 3 - c if c in (1, 2) else 4 * (r ^ 1) + c) for r in range(4) for c in range(4)])
        return token

    def add_crossed(j, token):
        def function(part, other):
            return [(part[...] + other[...].astype(F32)).astype(BF16)]

        sent, token = step(function, [short], [parts[3 - j], crossed[j]], token)
        went[j] = lax.ppermute(sent, "col", [(1, 0), (2, 3)])
        return token

    def finish(j, token):
        def function(part, inner, outer):
            other = jnp.where(is_inner(), inner[...], outer[...])
            return [(part[...] + other.astype(F32)).astype(BF16)]

        return step(function, [short], [known[j], crossed[3 - j], went[3 - j]], token)

    def inward(sent):
        return lax.ppermute(sent, "col", [(0, 1), (3, 2)])

    def project_own(values, basis):
        total = dot(values[...], basis[...])
        return total, total.astype(BF16)

    def project_beside(here, there, own, basis):
        total = dot(both_halves(here[...], there[...], lax.axis_index("row") % 2), basis[...])
        inner = is_inner()
        return jnp.where(inner, total, own[...]), jnp.where(inner, own[...], total), total.astype(BF16)

    def project_others(here, there, basis):
        straight = is_inner() == (lax.axis_index("row") % 2 == 0)
        one = dot(jnp.where(straight, here[...], there[...]), basis[...])
        two = dot(jnp.where(straight, there[...], here[...]), basis[...])
        return one, two, one.astype(BF16), two.astype(BF16)

    def project_act(values, basis, other):
        total = dot(values[:, :depth], basis[...]) + dot(values[:, depth:], other[...])
        return total, total.astype(BF16)

    def add_there(total, other):
        return [(total[...] + other[...].astype(F32)).astype(BF16)]

    other_basis = by_xor(input_basis, "row", 1)
    def same(value):
        return [value[...]]

    beside, distant, own, token = cut_gradients(gradients, depth)
    beside = by_xor(beside, "col", 1)
    distant = lax.ppermute(
        distant,
        ("row", "col"),
        [(4 * r + c, 4 * r + (c ^ 2 if r % 2 else 3 - c)) for r in range(4) for c in range(4)],
    )
    own_part, sent, token = step(project_own, [wide, short], [own, output_basis], token)
    came[0] = inward(sent)
    far, mine, token = cut_activations(activations, depth, token)
    far = by_xor(far, "row", 2)
    beside, token = step(same, [piece], [beside], token)
    distant, token = step(same, [piece], [distant], token)
    distant_there = by_xor(distant, "row", 2)
    one, two, sent, token = step(
        project_beside,
        [wide, wide, short],
        [beside, by_xor(beside, "row", 1), own_part, output_basis],
        token,
        after=[other_basis],
    )
    parts += [one, two]
    came[1] = inward(sent)
    token = add_inward(0, token)
    distant, token = step(
        lambda here, there: [both_halves(here[...], there[...], lax.axis_index("row") // 2)],
        [block],
        [distant, distant_there],
        token,
    )
    one, two, one_sent, two_sent, token = step(
        project_others,
        [wide, wide, short, short],
        [distant, by_xor(distant, "row", 1), output_basis],
        token,
    )
    parts += [one, two]
    came[2], came[3] = inward(one_sent), inward(two_sent)
    late = [None] * 4
    near_sum, sent, token = step(
        project_act, [wide, short], [mine, input_basis, other_basis], token
    )
    near_there = by_xor(sent, "row", 2)
    token = add_inward(1, token)
    token = add_crossed(0, token)
    far_sum, sent, token = step(project_act, [wide, short], [far, input_basis, other_basis], token)
    far_there = by_xor(sent, "row", 2)
    token = add_inward(2, token)
    token = add_crossed(1, token)
    far, token = step(add_there, [short], [far_sum, near_there], token)
    far_other = by_xor(far, "row", 1)
    token = add_inward(3, token)
    late[3], token = finish(3, token)
    near, token = step(add_there, [short], [near_sum, far_there], token)
    near_other = by_xor(near, "row", 1)
    token = add_crossed(2, token)
    late[2], token = finish(2, token)
    token = add_crossed(3, token)
    late[1], token = finish(1, token)
    turned, places, token = turn([near, far, near_other, far_other], seq_ids, token)
    return correct(turned, places, late[1:], known[0], crossed[3], went[3])


def on_device(rows, cols, activations, gradients, input_basis, output_basis, seq_ids):
    total = seq_ids.shape[0]
    if rows != 4 or cols != 4 or not total // 2 + 16 <= 2 * NARROW <= total:
        act_panel = project_any(activations, input_basis, "row")
        grad_panel = project_any(gradients, output_basis, "col")
        return correct_any(act_panel, grad_panel, seq_ids)
    return run(activations, gradients, input_basis, output_basis, seq_ids)


def solution(mesh):
    return jax.shard_map(
        functools.partial(on_device, mesh.shape["row"], mesh.shape["col"]),
        mesh=mesh,
        in_specs=(
            P(("grp", "row"), None),
            P(("grp", "col"), None),
            P(("grp", "row"), "col"),
            P(("grp", "col"), "row"),
            P("grp"),
        ),
        out_specs=P(("grp", "col"), "row"),
        check_vma=False,
    )
```
